32 devices in a mesh: lat: 4 (over x, core), lon: 8 (over z, y).
Axes of the slice: x: 2, y: 2, z: 4, core: 2. Of those that a mesh axis runs over, the one named last changes fastest.
Arguments:
- queries: bfloat16 [8192, 1024], P(('lat', 'lon')), may hold values from -6 to 6
- gain: bfloat16 [1024], replicated, may hold values from 0.099609375 to 1.8984375
- w_query: bfloat16 [1024, 1024], P('lon'), may hold values from -0.1875 to 0.1875
- w_out: bfloat16 [1024, 1024], P(None, 'lon'), may hold values from -0.75 to 0.75
- kv_cache: bfloat16 [2, 8, 256, 1024], P(None, 'lat'), may hold values from -60 to 60
- nbr_lists: int32 [32, 4], P(('lat', 'lon')), may hold values from 0 to 7, as said below
- counts: int32 [32], P(('lat', 'lon')), may hold values from 1 to 4, as said below
Outputs:
- decoded: bfloat16 [8192, 1024], P(('lat', 'lon'))
The draws below stay inside these ranges and needn't reach their ends.
Inputs may be any that keep to these rules, and one draw needn't show every extreme that they name: `nbr_lists`: query block b lies in band b // 8; band k holds latent blocks k * 2 to (k+1) * 2 - 1. Entries of b's list lie in its band or the bands beside it; its first counts[b] entries differ, the others repeat entry 0. `counts`: query blocks of the first and last band have 4 valid slots.
All inputs are finite; a program needn't handle non-finite values.
Results may differ from the reference program's by a relative error of at most 0.007.
The reference program's roundings to bfloat16 on the way count: a program that leaves them out, or rounds other values in their place, can miss the bound.
Values may be sent and summed in bfloat16 or wider, within the bound.
A program may use at most 64 MiB of HBM per device.

```python
import jax
import jax.numpy as jnp
from jax import lax

MODEL_WIDTH = 1024
H = 16
HD = 64
BLOCK_TOKENS = 256
NBR = 4
BLK_DEV = 2
QB_DEV = 1
NQB = 32
TOKENS = 8192
LATENT_BLOCKS = 8
N_LAT = 4
N_LON = 8


def neighbour_tables(key):
    list_key, count_key = jax.random.split(jax.random.fold_in(key, 7))
    query_ids = jnp.arange(NQB, dtype=jnp.int32)
    band_of = query_ids // (QB_DEV * N_LON)
    lower = jnp.maximum(band_of - 1, 0)
    upper = jnp.minimum(band_of + 1, N_LAT - 1)
    span_blocks = (upper - lower + 1) * BLK_DEV
    positions = jnp.arange(3 * BLK_DEV, dtype=jnp.int32)
    ranking = jax.random.randint(list_key, (NQB, 3 * BLK_DEV), 0, 2 ** 20, dtype=jnp.int32) * 64 + positions[None, :]
    ranking = jnp.where(positions[None, :] < span_blocks[:, None], ranking, 2 ** 30)
    picked = jnp.argsort(ranking, axis=1, stable=True)[:, :NBR].astype(jnp.int32)
    polar = (band_of == 0) | (band_of == N_LAT - 1)
    drawn_counts = jax.random.randint(count_key, (NQB,), 1, NBR + 1, dtype=jnp.int32)
    valid_counts = jnp.where(polar, NBR, drawn_counts).astype(jnp.int32)
    entries = lower[:, None] * BLK_DEV + picked
    slot_ids = jnp.arange(NBR, dtype=jnp.int32)
    entries = jnp.where(slot_ids[None, :] < valid_counts[:, None], entries, entries[:, :1])
    return (entries.astype(jnp.int32), valid_counts)


def draw_nbr_lists(key, part):
    return neighbour_tables(key)[0]


def draw_counts(key, part):
    return neighbour_tables(key)[1]


def draw_kv_cache(key, part):
    key_part, value_part = jax.random.split(jax.random.fold_in(key, 11), 2)
    array_shape = (LATENT_BLOCKS, BLOCK_TOKENS, MODEL_WIDTH)
    key_data = 1.5 * jax.random.truncated_normal(key_part, -4.0, 4.0, array_shape, jnp.float32)
    value_data = jax.random.truncated_normal(value_part, -4.0, 4.0, array_shape, jnp.float32)
    return jnp.stack([key_data, value_data]).astype(jnp.bfloat16)


def steps_of(stream_key, dims, pieces, least, high):
    def one(axis_at, shards_of):
        steps = jax.random.uniform(jax.random.fold_in(jax.random.fold_in(stream_key, 6), axis_at), (shards_of,), jnp.float32, least / len(pieces), high / len(pieces))
        return jnp.repeat(jnp.exp(steps), dims[axis_at] // shards_of).reshape((-1,) + (1,) * (len(dims) - axis_at - 1))

    level = one(*pieces[0])
    for cut in pieces[1:]:
        level = level * one(*cut)
    return level


def gaussian(key, dims, scale, most, cuts=(), held_as=jnp.bfloat16):
    drawn = scale * jax.random.normal(key, dims, jnp.float32)
    if cuts:
        drawn = drawn * steps_of(key, dims, cuts, -0.22, 0.18)
    return jnp.clip(drawn, -most, most).astype(held_as)


def setup_inputs(seed: int = 0) -> dict:
    key_list = jax.random.split(jax.random.key(seed), 8)
    queries = gaussian(key_list[0], (TOKENS, MODEL_WIDTH), 1.0, 6.0, ((0, 32),))
    gain = jnp.clip(1.0 + 0.18 * jax.random.normal(key_list[1], (MODEL_WIDTH,), jnp.float32), 0.099609375, 1.8984375).astype(jnp.bfloat16)
    w_query = gaussian(key_list[2], (MODEL_WIDTH, MODEL_WIDTH), MODEL_WIDTH ** -0.5, 0.1875, ((0, 8),))
    w_out = gaussian(key_list[3], (MODEL_WIDTH, MODEL_WIDTH), (MODEL_WIDTH // 16) ** -0.5, 0.75, ((1, 8),))
    kv_cache = draw_kv_cache(jax.random.fold_in(key_list[7], 71), 0)
    nbr_lists = draw_nbr_lists(jax.random.fold_in(key_list[7], 71), 0)
    counts = draw_counts(jax.random.fold_in(key_list[7], 71), 0)
    return dict(queries=queries, gain=gain, w_query=w_query, w_out=w_out, kv_cache=kv_cache, nbr_lists=nbr_lists, counts=counts)


def reference(queries, gain, w_query, w_out, kv_cache, nbr_lists, counts):
    rows = queries.astype(jnp.float32)
    rowwise_scale = lax.rsqrt(lax.optimization_barrier(jnp.mean(rows * rows, axis=1, keepdims=True)) + 1e-05)
    normed = (rows * rowwise_scale * gain.astype(jnp.float32)[None, :]).astype(jnp.bfloat16)
    query = (jnp.dot(normed, w_query, preferred_element_type=jnp.float32) * HD ** (-0.5)).astype(jnp.bfloat16)
    query_blocks = query.reshape(NQB, BLOCK_TOKENS, H, HD)
    slot_ids = jnp.arange(NBR, dtype=jnp.int32)

    def attend(inputs):
        q_block, listed, count_one = inputs
        key_rows = jnp.take(kv_cache[0], listed, axis=0).reshape(NBR * BLOCK_TOKENS, H, HD).astype(jnp.float32)
        value_rows = jnp.take(kv_cache[1], listed, axis=0).reshape(NBR * BLOCK_TOKENS, H, HD).astype(jnp.float32)
        scores = jnp.einsum('qhd,khd->qhk', q_block.astype(jnp.float32), key_rows)
        live_keys = jnp.repeat(slot_ids < count_one, BLOCK_TOKENS)
        scores = jnp.where(live_keys[None, None, :], scores, -jnp.inf)
        peak = lax.optimization_barrier(jnp.max(scores, axis=2, keepdims=True))
        expo = jnp.exp(scores - peak)
        total = lax.optimization_barrier(jnp.sum(expo, axis=2, keepdims=True))
        rounded = lax.optimization_barrier(expo.astype(jnp.bfloat16)).astype(jnp.float32)
        mixed = jnp.einsum('qhk,khd->qhd', rounded, value_rows)
        return (mixed / total).astype(jnp.bfloat16)
    attended = lax.map(attend, (query_blocks, nbr_lists, counts)).reshape(TOKENS, MODEL_WIDTH)
    return jnp.dot(attended, w_out, preferred_element_type=jnp.float32).astype(jnp.bfloat16)
```

```python
import functools

import jax
import jax.numpy as jnp
from jax import lax
from jax.experimental import pallas as pl
from jax.experimental.pallas import tpu as pltpu
from jax.sharding import PartitionSpec as P

H = 16
HD = 64
PAIR = 2 * HD
BLOCK_TOKENS = 256
MESH = pl.DeviceIdType.MESH
LOW = -1e30


def remote(src, dst, send_sem, recv_sem, device):
    return pltpu.make_async_remote_copy(
        src_ref=src, dst_ref=dst, send_sem=send_sem, recv_sem=recv_sem, device_id=device, device_id_type=MESH
    )


def kernel(
    n_lat, n_z, n_y,
    lists_ref, counts_ref, queries_ref, gain_ref, wq_ref, wo_ref, kv_ref,
    out_ref,
    wq_all, wo_all, kv_own, kv_chip, kv_far, normed, heads, best, total, running, attended,
    own_sems, kv_send, kv_recv, wq_z, wq_y, wq_core, wq_recv, wo_z, wo_y, wo_core, wo_recv,
):
    n_lon = n_z * n_y
    lat, lon = lax.axis_index("lat"), lax.axis_index("lon")
    z, y, core = lon // n_y, lon % n_y, lat % 2
    mate = lat + 1 - 2 * core
    far = lat - 1 + 2 * core
    has_far = jnp.logical_and(far >= 0, far < n_lat)
    far_safe = jnp.clip(far, 0, n_lat - 1)
    pairs = H // 2
    rows = queries_ref.shape[0]
    depth, columns = wq_ref.shape[0], wo_ref.shape[1]
    half_q, half_o = depth // 2, wo_ref.shape[0] // 2
    blocks = kv_ref.shape[1]

    own_copies = [
        pltpu.make_async_copy(wq_ref, wq_all.at[pl.ds(pl.multiple_of(lon * depth, depth), depth)], own_sems.at[0]),
        pltpu.make_async_copy(wo_ref, wo_all.at[lon], own_sems.at[1]),
        pltpu.make_async_copy(kv_ref, kv_own, own_sems.at[2]),
    ]
    for copy in own_copies:
        copy.start()

    z_peers = [lax.rem(z + d, n_z) * n_y + y for d in range(1, n_z)]
    y_peers = [z * n_y + lax.rem(y + d, n_y) for d in range(1, n_y)]
    barrier = pltpu.get_barrier_semaphore()
    for peer in z_peers + y_peers:
        pl.semaphore_signal(barrier, inc=1, device_id=(lat, peer), device_id_type=MESH)
    pl.semaphore_signal(barrier, inc=1, device_id=(mate, lon), device_id_type=MESH)

    @pl.when(has_far)
    def _():
        pl.semaphore_signal(barrier, inc=1, device_id=(far_safe, lon), device_id_type=MESH)

    pl.semaphore_wait(barrier, n_z - 1 + n_y - 1 + 1 + has_far.astype(jnp.int32))

    def wq_part(piece, half):
        return wq_all.at[pl.ds(pl.multiple_of(piece * depth + half * half_q, half_q), half_q)]

    def wo_part(piece, half):
        return wo_all.at[piece, pl.ds(pl.multiple_of(half * half_o, half_o), half_o)]

    wq_mine = wq_ref.at[pl.ds(pl.multiple_of(core * half_q, half_q), half_q)]
    wo_mine = wo_ref.at[pl.ds(pl.multiple_of(core * half_o, half_o), half_o)]
    w_query = (wq_part, wq_mine, wq_z, wq_y, wq_core, wq_recv)
    w_out = (wo_part, wo_mine, wo_z, wo_y, wo_core, wo_recv)

    def send_y(weight, piece_z, src):
        part, _, _, y_sems, _, recv = weight
        piece = piece_z * n_y + y
        for d, peer in enumerate(y_peers):
            remote(src, part(piece, core), y_sems.at[piece_z, d], recv.at[piece, core], (lat, peer)).start()

    def send_first(weight):
        part, mine, z_sems, _, _, recv = weight
        send_y(weight, z, mine)
        for d, peer in enumerate(z_peers):
            remote(mine, part(lon, core), z_sems.at[d], recv.at[lon, core], (lat, peer)).start()

    def arrived(weight, piece, half):
        part, _, _, _, core_sems, recv = weight
        ref = part(piece, half)
        remote(ref, ref, core_sems.at[piece], recv.at[piece, half], (mate, lon)).wait_recv()
        return ref

    def send_core(weight, piece, ref):
        part, _, _, _, core_sems, recv = weight
        remote(ref, part(piece, core), core_sems.at[piece], recv.at[piece, core], (mate, lon)).start()

    def pass_z(weight):
        for d in range(1, n_z):
            piece_z = lax.rem(z + n_z - d, n_z)
            piece = piece_z * n_y + y
            ref = arrived(weight, piece, core)
            send_y(weight, piece_z, ref)
            send_core(weight, piece, ref)

    def pass_y(weight):
        for k in range(n_z):
            piece_z = lax.rem(z + n_z - k, n_z)
            for d in range(1, n_y):
                piece = piece_z * n_y + lax.rem(y + n_y - d, n_y)
                send_core(weight, piece, arrived(weight, piece, core))

    def finish(weight):
        for d in range(1, n_lon):
            arrived(weight, lax.rem(lon + d, n_lon), 1 - core)

    def drain(weight):
        part, mine, z_sems, y_sems, core_sems, recv = weight
        for d, peer in enumerate(z_peers):
            remote(mine, part(lon, core), z_sems.at[d], recv.at[lon, core], (lat, peer)).wait_send()
        for k in range(n_z):
            for d, peer in enumerate(y_peers):
                remote(mine, part(lon, core), y_sems.at[k, d], recv.at[lon, core], (lat, peer)).wait_send()
        for d in range(1, n_lon):
            piece = lax.rem(lon + d, n_lon)
            remote(mine, part(lon, core), core_sems.at[piece], recv.at[lon, core], (mate, lon)).wait_send()

    def kv_copy(to_far, block, kind):
        target = kv_far if to_far else kv_chip
        index = (1 if to_far else 0, block, kind)
        return remote(
            kv_ref.at[kind, block], target.at[kind, block], kv_send.at[index], kv_recv.at[index],
            (far_safe if to_far else mate, lon),
        )

    send_first(w_query)
    for block in range(blocks):
        for kind in range(2):
            kv_copy(False, block, kind).start()

    @pl.when(has_far)
    def _():
        for block in range(blocks):
            for kind in range(2):
                kv_copy(True, block, kind).start()

    tokens = queries_ref[...].astype(jnp.float32)
    scale = lax.rsqrt(jnp.mean(tokens * tokens, axis=1, keepdims=True) + 1e-5)
    normed[...] = (tokens * scale * gain_ref[...].astype(jnp.float32)).astype(jnp.bfloat16)

    pass_z(w_query)
    pass_y(w_query)
    finish(w_query)
    send_first(w_out)
    own_copies[0].wait()

    lane = lax.broadcasted_iota(jnp.int32, (rows, PAIR), 1)

    @pl.loop(0, pairs // 2)
    def _(step):
        at = pl.multiple_of(step * 2 * PAIR, 2 * PAIR)
        made = jnp.dot(normed[...], wq_all[:, pl.ds(at, 2 * PAIR)], preferred_element_type=jnp.float32)
        made = made * HD ** (-0.5)
        for side in range(2):
            both = made[:, side * PAIR : (side + 1) * PAIR]
            heads[2 * step + side, :rows] = jnp.where(lane < HD, both, 0.0).astype(jnp.bfloat16)
            heads[2 * step + side, rows:] = jnp.where(lane < HD, 0.0, both).astype(jnp.bfloat16)

    def is_listed(block):
        found = jnp.logical_and(lists_ref[0, 0] == block, 0 < counts_ref[0])
        for slot in range(1, lists_ref.shape[1]):
            found = jnp.logical_or(
                found, jnp.logical_and(lists_ref[0, slot] == block, slot < counts_ref[0])
            )
        return found

    def attend(kv, band, which, first):
        live = [is_listed(band * blocks + b) for b in which]

        @pl.loop(0, pairs)
        def _(pair):
            at = pl.ds(pl.multiple_of(pair * PAIR, PAIR), PAIR)
            for part in range(2):
                here = pl.ds(part * rows, rows)
                q = heads[pair, here]
                scores = [
                    lax.dot_general(
                        q, kv[0, b, :, at], (((1,), (1,)), ((), ())), preferred_element_type=jnp.float32
                    )
                    for b in which
                ]
                peak = None if first else best[pair, here][:, :1]
                for s, alive in zip(scores, live):
                    top = jnp.where(alive, jnp.max(s, axis=1, keepdims=True), LOW)
                    peak = jnp.maximum(top, LOW) if peak is None else jnp.maximum(peak, top)
                added, mixed = None, None
                for s, alive, b in zip(scores, live, which):
                    weights = jnp.exp(s - jnp.where(alive, peak, jnp.inf))
                    lanes = weights[:, :128]
                    for k in range(1, BLOCK_TOKENS // 128):
                        lanes = lanes + weights[:, k * 128 : (k + 1) * 128]
                    product = jnp.dot(
                        weights.astype(jnp.bfloat16), kv[1, b, :, at], preferred_element_type=jnp.float32
                    )
                    added = lanes if added is None else added + lanes
                    mixed = product if mixed is None else mixed + product
                if first:
                    total[pair, here] = added
                    running[pair, here] = mixed
                else:
                    rescale = jnp.exp(best[pair, here][:, :1] - peak)
                    total[pair, here] = total[pair, here] * rescale + added
                    running[pair, here] = running[pair, here] * rescale + mixed
                best[pair, here] = jnp.broadcast_to(peak, (rows, PAIR))

    own_copies[2].wait()
    attend(kv_own, lat, range(blocks), True)
    pass_z(w_out)
    for block in range(blocks):
        for kind in range(2):
            kv_copy(False, block, kind).wait()
    attend(kv_chip, mate, range(blocks), False)
    pass_y(w_out)

    @pl.when(has_far)
    def _():
        for block in range(blocks):
            for kind in range(2):
                kv_copy(True, block, kind).wait()
            attend(kv_far, far_safe, [block], False)

    @pl.loop(0, pairs)
    def _(pair):
        at = pl.ds(pl.multiple_of(pair * PAIR, PAIR), PAIR)
        parts = []
        for part in range(2):
            here = pl.ds(part * rows, rows)
            parts.append(running[pair, here] / jnp.sum(total[pair, here], axis=1, keepdims=True))
        attended[:, at] = jnp.where(lane < HD, parts[0], parts[1]).astype(jnp.bfloat16)

    finish(w_out)
    own_copies[1].wait()
    group = max(1, 256 // columns)
    for step in range(n_lon // group):
        weight = jnp.concatenate([wo_all[step * group + k] for k in range(group)], axis=1)
        made = jnp.dot(attended[...], weight, preferred_element_type=jnp.float32)
        out_ref[:, step * group * columns : (step + 1) * group * columns] = made.astype(jnp.bfloat16)
    drain(w_query)
    drain(w_out)


def solution(mesh):
    n_lat, n_lon = mesh.shape["lat"], mesh.shape["lon"]
    n_y = 1
    while n_y * n_y * 4 <= n_lon:
        n_y *= 2
    n_z = n_lon // n_y

    def on_device(queries, gain, w_query, w_out, kv_cache, nbr_lists, counts):
        rows, width = queries.shape
        depth, columns = w_query.shape[0], w_out.shape[1]
        blocks = kv_cache.shape[1]
        vmem = pl.BlockSpec(memory_space=pltpu.VMEM)
        smem = pl.BlockSpec(memory_space=pltpu.SMEM)
        anywhere = pl.BlockSpec(memory_space=pl.ANY)
        dma = pltpu.SemaphoreType.DMA
        weight_sems = [dma((max(n_z - 1, 1),)), dma((n_z, max(n_y - 1, 1))), dma((n_lon,)), dma((n_lon, 2))]
        state = pltpu.VMEM((H // 2, 2 * rows, PAIR), jnp.float32)
        return pl.pallas_call(
            functools.partial(kernel, n_lat, n_z, n_y),
            out_shape=jax.ShapeDtypeStruct((rows, width), jnp.bfloat16),
            in_specs=[smem, smem, vmem, vmem, anywhere, anywhere, anywhere],
            out_specs=vmem,
            scratch_shapes=[
                pltpu.VMEM((width, width), jnp.bfloat16),
                pltpu.VMEM((n_lon, width, columns), jnp.bfloat16),
                pltpu.VMEM(kv_cache.shape, jnp.bfloat16),
                pltpu.VMEM(kv_cache.shape, jnp.bfloat16),
                pltpu.VMEM(kv_cache.shape, jnp.bfloat16),
                pltpu.VMEM((rows, width), jnp.bfloat16),
                pltpu.VMEM((H // 2, 2 * rows, PAIR), jnp.bfloat16),
                state,
                state,
                state,
                pltpu.VMEM((rows, width), jnp.bfloat16),
                dma((3,)),
                dma((2, blocks, 2)),
                dma((2, blocks, 2)),
                *weight_sems,
                *weight_sems,
            ],
            compiler_params=pltpu.CompilerParams(
                collective_id=0, has_side_effects=True, vmem_limit_bytes=48 * 1024 * 1024
            ),
        )(nbr_lists, counts, queries, gain.reshape(1, width), w_query, w_out, kv_cache)

    placed = (
        P(("lat", "lon"), None),
        P(),
        P("lon", None),
        P(None, "lon"),
        P(None, "lat", None, None),
        P(("lat", "lon"), None),
        P(("lat", "lon")),
    )
    return jax.shard_map(
        on_device, mesh=mesh, in_specs=placed, out_specs=P(("lat", "lon"), None), check_vma=False
    )
```

```python
import functools

import jax
import jax.numpy as jnp
from jax import lax
from jax.experimental import pallas as pl
from jax.experimental.pallas import tpu as pltpu
from jax.sharding import PartitionSpec as P

H = 16
HD = 64
PAIR = 2 * HD
BLOCK_TOKENS = 256
MESH = pl.DeviceIdType.MESH
LOW = -1e30


def remote(src, dst, send_sem, recv_sem, device):
    return pltpu.make_async_remote_copy(
        src_ref=src, dst_ref=dst, send_sem=send_sem, recv_sem=recv_sem, device_id=device, device_id_type=MESH
    )


def kernel(
    n_lat, n_z, n_y,
    lists_hbm, counts_hbm, queries_hbm, gain_hbm, wq_ref, wo_ref, kv_ref,
    out_ref,
    lists_ref, counts_ref, queries_ref, gain_ref, wq_all, wo_all, kv_own, kv_chip, kv_far, normed, heads, best, total, running, attended,
    own_sems, kv_send, kv_recv, wq_z, wq_y, wq_core, wq_recv, wo_z, wo_y, wo_core, wo_recv,
):
    n_lon = n_z * n_y
    lat, lon = lax.axis_index("lat"), lax.axis_index("lon")
    z, y, core = lon // n_y, lon % n_y, lat % 2
    mate = lat + 1 - 2 * core
    far = lat - 1 + 2 * core
    has_far = jnp.logical_and(far >= 0, far < n_lat)
    far_safe = jnp.clip(far, 0, n_lat - 1)
    pairs = H // 2
    rows = queries_ref.shape[0]
    depth, columns = wq_ref.shape[0], wo_ref.shape[1]
    half_q, half_o = depth // 2, wo_ref.shape[0] // 2
    blocks = kv_ref.shape[1]

    own_copies = [
        pltpu.make_async_copy(wq_ref, wq_all.at[pl.ds(pl.multiple_of(lon * depth, depth), depth)], own_sems.at[0]),
        pltpu.make_async_copy(wo_ref, wo_all.at[lon], own_sems.at[1]),
        pltpu.make_async_copy(kv_ref, kv_own, own_sems.at[2]),
        pltpu.make_async_copy(queries_hbm, queries_ref, own_sems.at[3]),
        pltpu.make_async_copy(gain_hbm, gain_ref, own_sems.at[4]),
        pltpu.make_async_copy(lists_hbm, lists_ref, own_sems.at[5]),
        pltpu.make_async_copy(counts_hbm, counts_ref, own_sems.at[6]),
    ]
    for copy in own_copies:
        copy.start()

    above, below = z + 1 < n_z, z > 0
    lon_up, lon_down = jnp.minimum(lon + n_y, n_lon - 1), jnp.maximum(lon - n_y, 0)
    y_peers = [z * n_y + lax.rem(y + d, n_y) for d in range(1, n_y)]
    barrier = pltpu.get_barrier_semaphore()
    for there, peer in ((above, lon_up), (below, lon_down)):

        @pl.when(there)
        def _(peer=peer):
            pl.semaphore_signal(barrier, inc=1, device_id=(lat, peer), device_id_type=MESH)

    for peer in y_peers:
        pl.semaphore_signal(barrier, inc=1, device_id=(lat, peer), device_id_type=MESH)
    pl.semaphore_signal(barrier, inc=1, device_id=(mate, lon), device_id_type=MESH)

    @pl.when(has_far)
    def _():
        pl.semaphore_signal(barrier, inc=1, device_id=(far_safe, lon), device_id_type=MESH)

    pl.semaphore_wait(barrier, n_y + sum(there.astype(jnp.int32) for there in (has_far, above, below)))

    def wq_part(piece, half):
        return wq_all.at[pl.ds(pl.multiple_of(piece * depth + half * half_q, half_q), half_q)]

    def wo_part(piece, half):
        return wo_all.at[piece, pl.ds(pl.multiple_of(half * half_o, half_o), half_o)]

    wq_mine = wq_ref.at[pl.ds(pl.multiple_of(core * half_q, half_q), half_q)]
    wo_mine = wo_ref.at[pl.ds(pl.multiple_of(core * half_o, half_o), half_o)]
    w_query = (wq_part, wq_mine, wq_z, wq_y, wq_core, wq_recv)
    w_out = (wo_part, wo_mine, wo_z, wo_y, wo_core, wo_recv)

    def send_y(weight, piece_z, src):
        part, _, _, y_sems, _, recv = weight
        piece = piece_z * n_y + y
        for d, peer in enumerate(y_peers):
            remote(src, part(piece, core), y_sems.at[piece_z, d], recv.at[piece, core], (lat, peer)).start()

    def z_copy(weight, piece_z, src, up):
        part, _, z_sems, _, _, recv = weight
        piece = piece_z * n_y + y
        peer = lon_up if up else lon_down
        return remote(
            src, part(piece, core), z_sems.at[piece_z, 0 if up else 1], recv.at[piece, core], (lat, peer)
        )

    def send_first(weight):
        mine = weight[1]

        @pl.when(above)
        def _():
            z_copy(weight, z, mine, True).start()

        @pl.when(below)
        def _():
            z_copy(weight, z, mine, False).start()

        send_y(weight, z, mine)

    def arrived(weight, piece, half):
        part, _, _, _, core_sems, recv = weight
        ref = part(piece, half)
        remote(ref, ref, core_sems.at[piece], recv.at[piece, half], (mate, lon)).wait_recv()
        return ref

    def send_core(weight, piece, ref):
        part, _, _, _, core_sems, recv = weight
        remote(ref, part(piece, core), core_sems.at[piece], recv.at[piece, core], (mate, lon)).start()

    def pass_z(weight):
        for d in range(1, n_z):
            for up, piece_z, there in ((True, z - d, z >= d), (False, z + d, z + d < n_z)):

                @pl.when(there)
                def _(up=up, piece_z=piece_z):
                    piece = piece_z * n_y + y
                    ref = arrived(weight, piece, core)

                    @pl.when(above if up else below)
                    def _():
                        z_copy(weight, piece_z, ref, up).start()

                    send_y(weight, piece_z, ref)
                    send_core(weight, piece, ref)

    def pass_y(weight):
        def pass_one(piece_z):
            for d in range(1, n_y):
                piece = piece_z * n_y + lax.rem(y + n_y - d, n_y)
                send_core(weight, piece, arrived(weight, piece, core))

        pass_one(z)
        for d in range(1, n_z):
            for piece_z, there in ((z - d, z >= d), (z + d, z + d < n_z)):

                @pl.when(there)
                def _(piece_z=piece_z):
                    pass_one(piece_z)

    def finish(weight):
        for d in range(1, n_lon):
            arrived(weight, lax.rem(lon + d, n_lon), 1 - core)

    def drain(weight):
        part, mine, z_sems, y_sems, core_sems, recv = weight
        for piece_z in range(n_z):

            @pl.when(jnp.logical_and(above, piece_z <= z))
            def _(piece_z=piece_z):
                z_copy(weight, piece_z, mine, True).wait_send()

            @pl.when(jnp.logical_and(below, piece_z >= z))
            def _(piece_z=piece_z):
                z_copy(weight, piece_z, mine, False).wait_send()

        for k in range(n_z):
            for d, peer in enumerate(y_peers):
                remote(mine, part(lon, core), y_sems.at[k, d], recv.at[lon, core], (lat, peer)).wait_send()
        for d in range(1, n_lon):
            piece = lax.rem(lon + d, n_lon)
            remote(mine, part(lon, core), core_sems.at[piece], recv.at[lon, core], (mate, lon)).wait_send()

    def kv_copy(to_far, block, kind):
        target = kv_far if to_far else kv_chip
        index = (1 if to_far else 0, block, kind)
        return remote(
            kv_ref.at[kind, block], target.at[kind, block], kv_send.at[index], kv_recv.at[index],
            (far_safe if to_far else mate, lon),
        )

    send_first(w_query)
    for block in range(blocks):
        for kind in range(2):
            kv_copy(False, block, kind).start()

    @pl.when(has_far)
    def _():
        for block in range(blocks):
            for kind in range(2):
                kv_copy(True, block, kind).start()

    own_copies[3].wait()
    own_copies[4].wait()
    tokens = queries_ref[...].astype(jnp.float32)
    scale = lax.rsqrt(jnp.mean(tokens * tokens, axis=1, keepdims=True) + 1e-5)
    normed[...] = (tokens * scale * gain_ref[...].astype(jnp.float32)).astype(jnp.bfloat16)

    pass_z(w_query)
    send_first(w_out)
    pass_y(w_query)
    finish(w_query)
    own_copies[0].wait()

    feature = lax.broadcasted_iota(jnp.int32, (PAIR, rows), 0)

    @pl.loop(0, pairs // 2)
    def _(step):
        at = pl.multiple_of(step * 2 * PAIR, 2 * PAIR)
        made = jnp.dot(normed[...], wq_all[:, pl.ds(at, 2 * PAIR)], preferred_element_type=jnp.float32)
        made = (made * HD ** (-0.5)).T
        for side in range(2):
            both = made[side * PAIR : (side + 1) * PAIR]
            heads[2 * step + side, :, :rows] = jnp.where(feature < HD, both, 0.0).astype(jnp.bfloat16)
            heads[2 * step + side, :, rows:] = jnp.where(feature < HD, 0.0, both).astype(jnp.bfloat16)

    own_copies[5].wait()
    own_copies[6].wait()

    def is_listed(block):
        found = jnp.logical_and(lists_ref[0, 0] == block, 0 < counts_ref[0])
        for slot in range(1, lists_ref.shape[1]):
            found = jnp.logical_or(
                found, jnp.logical_and(lists_ref[0, slot] == block, slot < counts_ref[0])
            )
        return found

    def attend(kv, band, first):
        live = [is_listed(band * blocks + b) for b in range(blocks)]

        @pl.loop(0, pairs)
        def _(pair):
            at = pl.ds(pl.multiple_of(pair * PAIR, PAIR), PAIR)
            values = [kv[1, b, :, at].T for b in range(blocks)]
            for part in range(2):
                q = heads[pair, :, part * rows : (part + 1) * rows]
                own = pl.ds(part * HD, HD)
                one = pl.ds(part, 1)
                scores = [
                    jnp.dot(kv[0, b, :, at], q, preferred_element_type=jnp.float32) for b in range(blocks)
                ]
                peak = jnp.full((1, rows), LOW, jnp.float32) if first else best[pair, one]
                for s, alive in zip(scores, live):
                    peak = jnp.maximum(peak, jnp.where(alive, jnp.max(s, axis=0, keepdims=True), LOW))
                added, mixed = 0.0, 0.0
                for s, alive, value in zip(scores, live, values):
                    weights = jnp.exp(s - jnp.where(alive, peak, jnp.inf))
                    added = added + jnp.sum(weights, axis=0, keepdims=True)
                    mixed = mixed + jnp.dot(
                        value[part * HD : (part + 1) * HD],
                        weights.astype(jnp.bfloat16),
                        preferred_element_type=jnp.float32,
                    )
                if not first:
                    rescale = jnp.exp(best[pair, one] - peak)
                    added = added + total[pair, one] * rescale
                    mixed = mixed + running[pair, own] * rescale
                best[pair, one] = peak
                total[pair, one] = added
                running[pair, own] = mixed

    own_copies[2].wait()
    attend(kv_own, lat, True)
    pass_z(w_out)
    for block in range(blocks):
        for kind in range(2):
            kv_copy(False, block, kind).wait()
    attend(kv_chip, mate, False)
    pass_y(w_out)

    @pl.when(has_far)
    def _():
        for block in range(blocks):
            for kind in range(2):
                kv_copy(True, block, kind).wait()
        attend(kv_far, far_safe, False)

    @pl.loop(0, pairs)
    def _(pair):
        at = pl.ds(pl.multiple_of(pair * PAIR, PAIR), PAIR)
        over = jnp.where(feature < HD, total[pair, 0:1], total[pair, 1:2])
        attended[:, at] = (running[pair] / over).T.astype(jnp.bfloat16)

    finish(w_out)
    own_copies[1].wait()
    group = max(1, 256 // columns)
    for step in range(n_lon // group):
        weight = jnp.concatenate([wo_all[step * group + k] for k in range(group)], axis=1)
        made = jnp.dot(attended[...], weight, preferred_element_type=jnp.float32)
        out_ref[:, step * group * columns : (step + 1) * group * columns] = made.astype(jnp.bfloat16)
    drain(w_query)
    drain(w_out)


def solution(mesh):
    n_lat, n_lon = mesh.shape["lat"], mesh.shape["lon"]
    n_y = 1
    while n_y * n_y * 4 <= n_lon:
        n_y *= 2
    n_z = n_lon // n_y

    def on_device(queries, gain, w_query, w_out, kv_cache, nbr_lists, counts):
        rows, width = queries.shape
        depth, columns = w_query.shape[0], w_out.shape[1]
        blocks = kv_cache.shape[1]
        vmem = pl.BlockSpec(memory_space=pltpu.VMEM)
        anywhere = pl.BlockSpec(memory_space=pltpu.HBM)
        dma = pltpu.SemaphoreType.DMA
        weight_sems = [dma((n_z, 2)), dma((n_z, max(n_y - 1, 1))), dma((n_lon,)), dma((n_lon, 2))]
        state = pltpu.VMEM((H // 2, 8, rows), jnp.float32)
        return pl.pallas_call(
            functools.partial(kernel, n_lat, n_z, n_y),
            out_shape=jax.ShapeDtypeStruct((rows, width), jnp.bfloat16),
            in_specs=[anywhere] * 7,
            out_specs=vmem,
            scratch_shapes=[
                pltpu.SMEM(nbr_lists.shape, jnp.int32),
                pltpu.SMEM(counts.shape, jnp.int32),
                pltpu.VMEM((rows, width), jnp.bfloat16),
                pltpu.VMEM((1, width), jnp.bfloat16),
                pltpu.VMEM((width, width), jnp.bfloat16),
                pltpu.VMEM((n_lon, width, columns), jnp.bfloat16),
                pltpu.VMEM(kv_cache.shape, jnp.bfloat16),
                pltpu.VMEM(kv_cache.shape, jnp.bfloat16),
                pltpu.VMEM(kv_cache.shape, jnp.bfloat16),
                pltpu.VMEM((rows, width), jnp.bfloat16),
                pltpu.VMEM((H // 2, PAIR, 2 * rows), jnp.bfloat16),
                state,
                state,
                pltpu.VMEM((H // 2, PAIR, rows), jnp.float32),
                pltpu.VMEM((rows, width), jnp.bfloat16),
                dma((7,)),
                dma((2, blocks, 2)),
                dma((2, blocks, 2)),
                *weight_sems,
                *weight_sems,
            ],
            compiler_params=pltpu.CompilerParams(
                collective_id=0, has_side_effects=True, vmem_limit_bytes=48 * 1024 * 1024
            ),
        )(nbr_lists, counts, queries, gain.reshape(1, width), w_query, w_out, kv_cache)

    placed = (
        P(("lat", "lon"), None),
        P(),
        P("lon", None),
        P(None, "lon"),
        P(None, "lat", None, None),
        P(("lat", "lon"), None),
        P(("lat", "lon")),
    )
    return jax.shard_map(
        on_device, mesh=mesh, in_specs=placed, out_specs=P(("lat", "lon"), None), check_vma=False
    )
```

```python
import functools

import jax
import jax.numpy as jnp
from jax import lax
from jax.experimental import pallas as pl
from jax.experimental.pallas import tpu as pltpu
from jax.sharding import PartitionSpec as P

H = 16
HD = 64
PAIR = 2 * HD
BLOCK_TOKENS = 256
MESH = pl.DeviceIdType.MESH
LOW = -1e30


def remote(src, dst, send_sem, recv_sem, device):
    return pltpu.make_async_remote_copy(
        src_ref=src, dst_ref=dst, send_sem=send_sem, recv_sem=recv_sem, device_id=device, device_id_type=MESH
    )


def kernel(
    n_lat, n_z, n_y,
    lists_hbm, counts_hbm, queries_hbm, gain_hbm, wq_ref, wo_ref, kv_ref,
    out_ref,
    lists_ref, counts_ref, queries_ref, gain_ref, wq_all, wo_all, kv_own, kv_chip, kv_far, normed, heads, best, total, running, attended,
    own_sems, kv_send, kv_recv, wq_z, wq_y, wq_core, wq_recv, wo_z, wo_y, wo_core, wo_recv,
):
    n_lon = n_z * n_y
    lat, lon = lax.axis_index("lat"), lax.axis_index("lon")
    z, y, core = lon // n_y, lon % n_y, lat % 2
    mate = lat + 1 - 2 * core
    far = lat - 1 + 2 * core
    has_far = jnp.logical_and(far >= 0, far < n_lat)
    far_safe = jnp.clip(far, 0, n_lat - 1)
    pairs = H // 2
    rows = queries_ref.shape[0]
    depth, columns = wq_ref.shape[0], wo_ref.shape[1]
    half_q, half_o = depth // 2, wo_ref.shape[0] // 2
    blocks = kv_ref.shape[1]

    own_copies = [
        pltpu.make_async_copy(wq_ref, wq_all.at[pl.ds(pl.multiple_of(lon * depth, depth), depth)], own_sems.at[0]),
        pltpu.make_async_copy(wo_ref, wo_all.at[lon], own_sems.at[1]),
        pltpu.make_async_copy(kv_ref, kv_own, own_sems.at[2]),
        pltpu.make_async_copy(queries_hbm, queries_ref, own_sems.at[3]),
        pltpu.make_async_copy(gain_hbm, gain_ref, own_sems.at[4]),
        pltpu.make_async_copy(lists_hbm, lists_ref, own_sems.at[5]),
        pltpu.make_async_copy(counts_hbm, counts_ref, own_sems.at[6]),
    ]
    for copy in own_copies:
        copy.start()

    above, below = z + 1 < n_z, z > 0
    lon_up, lon_down = jnp.minimum(lon + n_y, n_lon - 1), jnp.maximum(lon - n_y, 0)
    y_peers = [z * n_y + lax.rem(y + d, n_y) for d in range(1, n_y)]
    barrier = pltpu.get_barrier_semaphore()
    for there, peer in ((above, lon_up), (below, lon_down)):

        @pl.when(there)
        def _(peer=peer):
            pl.semaphore_signal(barrier, inc=1, device_id=(lat, peer), device_id_type=MESH)

    for peer in y_peers:
        pl.semaphore_signal(barrier, inc=1, device_id=(lat, peer), device_id_type=MESH)
    pl.semaphore_signal(barrier, inc=1, device_id=(mate, lon), device_id_type=MESH)

    @pl.when(has_far)
    def _():
        pl.semaphore_signal(barrier, inc=1, device_id=(far_safe, lon), device_id_type=MESH)

    pl.semaphore_wait(barrier, n_y + sum(there.astype(jnp.int32) for there in (has_far, above, below)))

    def wq_part(piece, half):
        return wq_all.at[pl.ds(pl.multiple_of(piece * depth + half * half_q, half_q), half_q)]

    def wo_part(piece, half):
        return wo_all.at[piece, pl.ds(pl.multiple_of(half * half_o, half_o), half_o)]

    wq_mine = wq_ref.at[pl.ds(pl.multiple_of(core * half_q, half_q), half_q)]
    wo_mine = wo_ref.at[pl.ds(pl.multiple_of(core * half_o, half_o), half_o)]
    w_query = (wq_part, wq_mine, wq_z, wq_y, wq_core, wq_recv)
    w_out = (wo_part, wo_mine, wo_z, wo_y, wo_core, wo_recv)

    def send_y(weight, piece_z, src):
        part, _, _, y_sems, _, recv = weight
        piece = piece_z * n_y + y
        for d, peer in enumerate(y_peers):
            remote(src, part(piece, core), y_sems.at[piece_z, d], recv.at[piece, core], (lat, peer)).start()

    def z_copy(weight, piece_z, src, up):
        part, _, z_sems, _, _, recv = weight
        piece = piece_z * n_y + y
        peer = lon_up if up else lon_down
        return remote(
            src, part(piece, core), z_sems.at[piece_z, 0 if up else 1], recv.at[piece, core], (lat, peer)
        )

    def send_first(weight):
        mine = weight[1]

        @pl.when(above)
        def _():
            z_copy(weight, z, mine, True).start()

        @pl.when(below)
        def _():
            z_copy(weight, z, mine, False).start()

        send_y(weight, z, mine)

    def arrived(weight, piece, half):
        part, _, _, _, core_sems, recv = weight
        ref = part(piece, half)
        remote(ref, ref, core_sems.at[piece], recv.at[piece, half], (mate, lon)).wait_recv()
        return ref

    def send_core(weight, piece, ref):
        part, _, _, _, core_sems, recv = weight
        remote(ref, part(piece, core), core_sems.at[piece], recv.at[piece, core], (mate, lon)).start()

    def pass_z(weight):
        for d in range(1, n_z):
            for up, piece_z, there in ((True, z - d, z >= d), (False, z + d, z + d < n_z)):

                @pl.when(there)
                def _(up=up, piece_z=piece_z):
                    piece = piece_z * n_y + y
                    ref = arrived(weight, piece, core)

                    @pl.when(above if up else below)
                    def _():
                        z_copy(weight, piece_z, ref, up).start()

                    send_y(weight, piece_z, ref)
                    send_core(weight, piece, ref)

    def pass_y(weight):
        def pass_one(piece_z):
            for d in range(1, n_y):
                piece = piece_z * n_y + lax.rem(y + n_y - d, n_y)
                send_core(weight, piece, arrived(weight, piece, core))

        pass_one(z)
        for d in range(1, n_z):
            for piece_z, there in ((z - d, z >= d), (z + d, z + d < n_z)):

                @pl.when(there)
                def _(piece_z=piece_z):
                    pass_one(piece_z)

    def finish(weight):
        for d in range(1, n_lon):
            arrived(weight, lax.rem(lon + d, n_lon), 1 - core)

    def drain(weight):
        part, mine, z_sems, y_sems, core_sems, recv = weight
        for piece_z in range(n_z):

            @pl.when(jnp.logical_and(above, piece_z <= z))
            def _(piece_z=piece_z):
                z_copy(weight, piece_z, mine, True).wait_send()

            @pl.when(jnp.logical_and(below, piece_z >= z))
            def _(piece_z=piece_z):
                z_copy(weight, piece_z, mine, False).wait_send()

        for k in range(n_z):
            for d, peer in enumerate(y_peers):
                remote(mine, part(lon, core), y_sems.at[k, d], recv.at[lon, core], (lat, peer)).wait_send()
        for d in range(1, n_lon):
            piece = lax.rem(lon + d, n_lon)
            remote(mine, part(lon, core), core_sems.at[piece], recv.at[lon, core], (mate, lon)).wait_send()

    def kv_copy(to_far, block, kind):
        target = kv_far if to_far else kv_chip
        index = (1 if to_far else 0, block, kind)
        return remote(
            kv_ref.at[kind, block], target.at[kind, block], kv_send.at[index], kv_recv.at[index],
            (far_safe if to_far else mate, lon),
        )

    send_first(w_query)
    for block in range(blocks):
        for kind in range(2):
            kv_copy(False, block, kind).start()

    @pl.when(has_far)
    def _():
        for block in range(blocks):
            for kind in range(2):
                kv_copy(True, block, kind).start()

    own_copies[3].wait()
    own_copies[4].wait()
    tokens = queries_ref[...].astype(jnp.float32)
    scale = lax.rsqrt(jnp.mean(tokens * tokens, axis=1, keepdims=True) + 1e-5)
    normed[...] = (tokens * scale * gain_ref[...].astype(jnp.float32)).astype(jnp.bfloat16)

    pass_z(w_query)
    send_first(w_out)
    pass_y(w_query)
    finish(w_query)
    own_copies[0].wait()

    feature = lax.broadcasted_iota(jnp.int32, (PAIR, rows), 0)

    @pl.loop(0, pairs // 2)
    def _(step):
        at = pl.multiple_of(step * 2 * PAIR, 2 * PAIR)
        made = jnp.dot(normed[...], wq_all[:, pl.ds(at, 2 * PAIR)], preferred_element_type=jnp.float32)
        made = (made * HD ** (-0.5)).T
        for side in range(2):
            both = made[side * PAIR : (side + 1) * PAIR]
            heads[2 * step + side, :, :rows] = jnp.where(feature < HD, both, 0.0).astype(jnp.bfloat16)
            heads[2 * step + side, :, rows:] = jnp.where(feature < HD, 0.0, both).astype(jnp.bfloat16)

    own_copies[5].wait()
    own_copies[6].wait()

    def is_listed(block):
        found = jnp.logical_and(lists_ref[0, 0] == block, 0 < counts_ref[0])
        for slot in range(1, lists_ref.shape[1]):
            found = jnp.logical_or(
                found, jnp.logical_and(lists_ref[0, slot] == block, slot < counts_ref[0])
            )
        return found

    def attend(kv, band, first):
        live = [is_listed(band * blocks + b) for b in range(blocks)]

        @pl.loop(0, pairs, unroll=4)
        def _(pair):
            at = pl.ds(pl.multiple_of(pair * PAIR, PAIR), PAIR)
            values = [kv[1, b, :, at].T for b in range(blocks)]
            for part in range(2):
                q = heads[pair, :, part * rows : (part + 1) * rows]
                own = pl.ds(part * HD, HD)
                one = pl.ds(part, 1)
                scores = [
                    jnp.dot(kv[0, b, :, at], q, preferred_element_type=jnp.float32) for b in range(blocks)
                ]
                peak = jnp.full((1, rows), LOW, jnp.float32) if first else best[pair, one]
                for s, alive in zip(scores, live):
                    peak = jnp.maximum(peak, jnp.where(alive, jnp.max(s, axis=0, keepdims=True), LOW))
                added, mixed = 0.0, 0.0
                for s, alive, value in zip(scores, live, values):
                    weights = jnp.exp(s - jnp.where(alive, peak, jnp.inf))
                    added = added + jnp.sum(weights, axis=0, keepdims=True)
                    mixed = mixed + jnp.dot(
                        value[part * HD : (part + 1) * HD],
                        weights.astype(jnp.bfloat16),
                        preferred_element_type=jnp.float32,
                    )
                if not first:
                    rescale = jnp.exp(best[pair, one] - peak)
                    added = added + total[pair, one] * rescale
                    mixed = mixed + running[pair, own] * rescale
                best[pair, one] = peak
                total[pair, one] = added
                running[pair, own] = mixed

    own_copies[2].wait()
    pass_z(w_out)
    attend(kv_own, lat, True)
    pass_y(w_out)
    for block in range(blocks):
        for kind in range(2):
            kv_copy(False, block, kind).wait()
    attend(kv_chip, mate, False)

    @pl.when(has_far)
    def _():
        for block in range(blocks):
            for kind in range(2):
                kv_copy(True, block, kind).wait()
        attend(kv_far, far_safe, False)

    @pl.loop(0, pairs)
    def _(pair):
        at = pl.ds(pl.multiple_of(pair * PAIR, PAIR), PAIR)
        over = jnp.where(feature < HD, total[pair, 0:1], total[pair, 1:2])
        attended[:, at] = (running[pair] / over).T.astype(jnp.bfloat16)

    finish(w_out)
    own_copies[1].wait()
    group = max(1, 256 // columns)
    for step in range(n_lon // group):
        weight = jnp.concatenate([wo_all[step * group + k] for k in range(group)], axis=1)
        made = jnp.dot(attended[...], weight, preferred_element_type=jnp.float32)
        out_ref[:, step * group * columns : (step + 1) * group * columns] = made.astype(jnp.bfloat16)
    drain(w_query)
    drain(w_out)


def solution(mesh):
    n_lat, n_lon = mesh.shape["lat"], mesh.shape["lon"]
    n_y = 1
    while n_y * n_y * 4 <= n_lon:
        n_y *= 2
    n_z = n_lon // n_y

    def on_device(queries, gain, w_query, w_out, kv_cache, nbr_lists, counts):
        rows, width = queries.shape
        depth, columns = w_query.shape[0], w_out.shape[1]
        blocks = kv_cache.shape[1]
        vmem = pl.BlockSpec(memory_space=pltpu.VMEM)
        anywhere = pl.BlockSpec(memory_space=pltpu.HBM)
        dma = pltpu.SemaphoreType.DMA
        weight_sems = [dma((n_z, 2)), dma((n_z, max(n_y - 1, 1))), dma((n_lon,)), dma((n_lon, 2))]
        state = pltpu.VMEM((H // 2, 8, rows), jnp.float32)
        return pl.pallas_call(
            functools.partial(kernel, n_lat, n_z, n_y),
            out_shape=jax.ShapeDtypeStruct((rows, width), jnp.bfloat16),
            in_specs=[anywhere] * 7,
            out_specs=vmem,
            scratch_shapes=[
                pltpu.SMEM(nbr_lists.shape, jnp.int32),
                pltpu.SMEM(counts.shape, jnp.int32),
                pltpu.VMEM((rows, width), jnp.bfloat16),
                pltpu.VMEM((1, width), jnp.bfloat16),
                pltpu.VMEM((width, width), jnp.bfloat16),
                pltpu.VMEM((n_lon, width, columns), jnp.bfloat16),
                pltpu.VMEM(kv_cache.shape, jnp.bfloat16),
                pltpu.VMEM(kv_cache.shape, jnp.bfloat16),
                pltpu.VMEM(kv_cache.shape, jnp.bfloat16),
                pltpu.VMEM((rows, width), jnp.bfloat16),
                pltpu.VMEM((H // 2, PAIR, 2 * rows), jnp.bfloat16),
                state,
                state,
                pltpu.VMEM((H // 2, PAIR, rows), jnp.float32),
                pltpu.VMEM((rows, width), jnp.bfloat16),
                dma((7,)),
                dma((2, blocks, 2)),
                dma((2, blocks, 2)),
                *weight_sems,
                *weight_sems,
            ],
            compiler_params=pltpu.CompilerParams(
                collective_id=0, has_side_effects=True, vmem_limit_bytes=60 * 1024 * 1024
            ),
        )(nbr_lists, counts, queries, gain.reshape(1, width), w_query, w_out, kv_cache)

    placed = (
        P(("lat", "lon"), None),
        P(),
        P("lon", None),
        P(None, "lon"),
        P(None, "lat", None, None),
        P(("lat", "lon"), None),
        P(("lat", "lon")),
    )
    return jax.shard_map(
        on_device, mesh=mesh, in_specs=placed, out_specs=P(("lat", "lon"), None), check_vma=False
    )
```
